32 devices in a mesh: groups: 2 (over x), ep: 16 (over z, y, core).
Axes of the slice: x: 2, y: 2, z: 4, core: 2. Of those that a mesh axis runs over, the one named last changes fastest.
Arguments:
- tokens: bfloat16 [1024, 3584], P(('groups', 'ep')), parts along dimension 0, may hold values from -6 to 6
- routes: int32 [1024, 8], P(('groups', 'ep')), parts along dimension 0, may hold values from 0 to 255, all different within a row; in each aligned block of 32 rows (0 to 31, 32 to 63, ...) at most 2 rows name the same one
- gate_num: int32 [1024, 8], P(('groups', 'ep')), parts along dimension 0, may hold values from 1 to 255
- w_gate: bfloat16 [16, 3584, 512], P('ep'), may hold values from -0.09375 to 0.09375
- w_up: bfloat16 [16, 3584, 512], P('ep'), may hold values from -0.09375 to 0.09375
- w_down: bfloat16 [16, 512, 3584], P('ep'), may hold values from -0.1875 to 0.1875
Outputs:
- combined: bfloat16 [1024, 3584], P(('groups', 'ep')), parts along dimension 0
The draws below stay inside these ranges and needn't reach their ends.
There are 2 independent parts, one for each index of `groups`. The reference program is written for one: setup_inputs(seed, part) draws one part's arguments, and reference() takes and returns one part's arrays. A program takes and returns all parts, laid end to end along the dimension named above; an argument that names none is the same for every part. Nothing has to cross between parts.
Inputs may be any that keep to these rules, and one draw needn't show every extreme that they name: `routes`: each row names 8 different experts; among the 32 rows of one device no expert is named more than 2 times, a bound that some block reaches.
All inputs are finite; a program needn't handle non-finite values.
Results may differ from the reference program's by a relative error of at most 0.0058.
Values may be sent and summed in bfloat16 or wider, within the bound.
A program may use at most 64 MiB of HBM per device.

```python
import math
import jax
import jax.numpy as jnp
import numpy as np
from jax import lax

D = 3584
FF = 1024
SPLIT = 2
FF_DEV = 512
TOPK = 8
EXPERTS = 256
TOK_DEV = 32
HELD = 8
TOKENS = 512
CAP = 2
N_EP = 16


def with_ends(drawn, rng, least, largest):
    shape = drawn.shape
    spot = [jax.random.randint(jax.random.fold_in(rng, axis), (), 0, shape[axis]) for axis in range(len(shape))]
    drawn = drawn.at[tuple(spot)].set(least)
    longest = shape.index(max(shape))
    spot[longest] = (spot[longest] + 1) % shape[longest]
    return drawn.at[tuple(spot)].set(largest)


def levels(stream_key, dims, pieces, least, high):
    loudness, own = 1.0, jax.random.fold_in(stream_key, 6)
    for dim, shards_of in pieces:
        steps = jnp.exp(jax.random.uniform(jax.random.fold_in(own, dim), (shards_of,), jnp.float32, least / len(pieces), high / len(pieces)))
        loudness = loudness * jnp.repeat(steps, dims[dim] // shards_of).reshape([-1 if axis == dim else 1 for axis in range(len(dims))])
    return loudness


def deal_out(rng, own, number, rows, amount, top, reach, slope):
    sequence = jax.random.permutation(rng, amount)
    crowded, common = load_shares(amount, rows * top, reach, slope, True), load_shares(amount, rows * top, reach, slope, False)
    places = jnp.arange(amount)

    def named(sizes, turn):
        used = int((sizes > 0).sum())
        fixed = max(1, used // 4)
        moved = fixed + (places - fixed + turn * (used - fixed)) % max(1, amount - fixed)
        return jnp.zeros((amount,), jnp.int32).at[sequence[jnp.where(places < fixed, places, moved)]].set(jnp.asarray(sizes, jnp.int32))

    sizes = jnp.where(number % 4 == 0, named(crowded, number // 4), named(common, number - number // 4 - 1))
    mixed = jax.random.permutation(jax.random.fold_in(own, 3), amount)
    giver, receiver = mixed[0:amount // 2 * 2:2], mixed[1:amount // 2 * 2:2]
    margin = jnp.minimum(sizes[giver] - 1, reach - sizes[receiver]) // 2
    margin = jnp.where((giver == sequence[0]) | (receiver == sequence[0]) | (sizes[receiver] == 0), 0, jnp.maximum(margin, 0))
    moved = jax.random.randint(jax.random.fold_in(own, 4), (amount // 2,), 0, 1 << 20) % (margin + 1)
    sizes = sizes.at[giver].add(-moved).at[receiver].add(moved)
    labels = jnp.searchsorted(jnp.cumsum(sizes), jnp.arange(rows * top), side="right").astype(jnp.int32)
    listing = labels.reshape(top, rows).T
    listing = listing[jax.random.permutation(jax.random.fold_in(own, 1), rows)]
    turn = jax.random.randint(jax.random.fold_in(own, 2), (rows, 1), 0, top)
    return jnp.take_along_axis(listing, (jnp.arange(top)[None, :] + turn) % top, axis=1)


def load_shares(amount, total, reach, skew, full):
    portions = [(1 << 20) // math.isqrt(rank ** skew) + 1 for rank in range(1, amount + 1)]
    largest = reach if full else min(reach, max(-(-total // amount), total * portions[0] // sum(portions)))
    least = 1 if total - largest >= amount - 1 else 0
    holding, surplus = [largest] + [least] * (amount - 1), total - largest - least * (amount - 1)
    while surplus > 0:
        movable = [i for i in range(1, amount) if holding[i] < largest] or [i for i in range(1, amount) if holding[i] < reach]
        whole, left = sum([portions[i] for i in movable]), surplus
        for i in movable:
            extra = min(reach - holding[i], max(1, left * portions[i] // whole), surplus)
            holding[i] = holding[i] + extra
            surplus = surplus - extra
    return np.array(holding)


def gaussian(key, extent, spread, limit, cuts=(), held_as=jnp.bfloat16):
    entries = spread * jax.random.normal(key, extent, jnp.float32)
    if cuts:
        entries = entries * levels(key, extent, cuts, -0.22, 0.18)
    return jnp.clip(entries, -limit, limit).astype(held_as)


def setup_inputs(seed: int = 0, part: int = 0) -> dict:
    key_of = jax.random.split(jax.random.key(seed), 7)
    own_keys = jax.random.split(jax.random.fold_in(key_of[6], part), 7)
    tokens = gaussian(own_keys[0], (TOKENS, D), 1.0, 6.0, ((0, 16),))
    routes_keys = jax.random.split(jax.random.fold_in(own_keys[1], 1), TOKENS // TOK_DEV)
    routes_turns = jax.random.permutation(jax.random.fold_in(own_keys[1], 3), TOKENS // TOK_DEV)
    routes = jax.vmap(lambda own, number: deal_out(jax.random.fold_in(own_keys[1], 2), own, number, TOK_DEV, EXPERTS, TOPK, CAP, 2))(routes_keys, routes_turns).reshape((TOKENS, TOPK))
    gate_num = with_ends(jax.random.randint(own_keys[2], (TOKENS, TOPK), 1, 256), jax.random.fold_in(own_keys[2], 1), 1, 255).astype(jnp.int32)
    w_gate = gaussian(key_of[3], (HELD * SPLIT, D, FF_DEV), D ** -0.5, 0.09375, ((0, 16),))
    w_up = gaussian(key_of[4], (HELD * SPLIT, D, FF_DEV), D ** -0.5, 0.09375, ((0, 16),))
    w_down = gaussian(key_of[5], (HELD * SPLIT, FF_DEV, D), FF ** -0.5, 0.1875, ((0, 16),))
    return dict(tokens=tokens, routes=routes, gate_num=gate_num, w_gate=w_gate, w_up=w_up, w_down=w_down)


def reference(tokens, routes, gate_num, w_gate, w_up, w_down):
    tok_total, top_count = routes.shape
    feature_width = tokens.shape[1]
    slot_total = N_EP * CAP
    expert_total = w_gate.shape[0] // SPLIT
    flat_routes = routes.reshape(-1).astype(jnp.int32)
    flat_gates = gate_num.reshape(-1).astype(jnp.float32) / 256.0
    gate_all = w_gate.reshape(expert_total, SPLIT, feature_width, w_gate.shape[2])
    up_all = w_up.reshape(expert_total, SPLIT, feature_width, w_up.shape[2])
    down_all = w_down.reshape(expert_total, SPLIT, w_down.shape[1], feature_width)

    def per_expert(combined, inputs):
        expert_id, gate_w, up_w, down_w = inputs
        chosen = flat_routes == expert_id
        slot_index = jnp.nonzero(chosen, size=slot_total, fill_value=0)[0].astype(jnp.int32)
        is_valid = jnp.arange(slot_total, dtype=jnp.int32) < jnp.sum(chosen.astype(jnp.int32))
        token_ids = slot_index // top_count
        row_block = jnp.where(is_valid[:, None], tokens[token_ids], jnp.zeros((), tokens.dtype))
        gate_scale = jnp.where(is_valid, flat_gates[slot_index], jnp.zeros((), jnp.float32))
        partial_value = jnp.zeros((slot_total, feature_width), jnp.float32)
        for piece in range(SPLIT):
            gate_part = jnp.dot(row_block, gate_w[piece], preferred_element_type=jnp.float32)
            up_part = jnp.dot(row_block, up_w[piece], preferred_element_type=jnp.float32)
            hidden = (jax.nn.silu(gate_part) * up_part).astype(jnp.bfloat16)
            partial_value = partial_value + jnp.dot(hidden, down_w[piece], preferred_element_type=jnp.float32)
        output = partial_value.astype(jnp.bfloat16)
        total = gate_scale[:, None] * output.astype(jnp.float32)
        combined = combined.at[token_ids].add(total)
        return combined, None

    start = jnp.zeros((tok_total, feature_width), jnp.float32)
    expert_ids = jnp.arange(expert_total, dtype=jnp.int32)
    combined, unused = lax.scan(per_expert, start, (expert_ids, gate_all, up_all, down_all))
    return combined.astype(jnp.bfloat16)
```

```python
import functools

import jax
import jax.numpy as jnp
from jax import lax
from jax.experimental import pallas as pl
from jax.experimental.pallas import tpu as pltpu
from jax.sharding import PartitionSpec as P

SPLIT = 2
CAP = 2
BLOCK = 256
TILE = 16
F32 = jnp.float32
BF16 = jnp.bfloat16


def iota(shape, dim):
    return lax.broadcasted_iota(jnp.int32, shape, dim)


def mm(a, b):
    return jnp.dot(a, b, preferred_element_type=F32)


def mm_nt(a, b):
    return lax.dot_general(a, b, (((1,), (1,)), ((), ())), preferred_element_type=F32)


def one_hot(cond):
    return jnp.where(cond, 1.0, 0.0).astype(BF16)


def kernel(
    n, group, tokens, routes, gates, wg_hbm, wu_hbm, wd_hbm, out,
    wg, wu, wd, send, recv, relayed, zsend, zrecv, rsend, ret,
    wsem, send_s, send_r, relay_s, relay_r, z_s, z_r, ret_s, ret_r,
):
    me = lax.axis_index("ep")
    side = lax.rem(me, SPLIT)
    partner = me + 1 - 2 * side
    rows, width = tokens.shape
    top = routes.shape[1]
    half = width // SPLIT
    blocks = half // BLOCK
    experts = n // SPLIT
    slots = experts * CAP

    loads = [
        pltpu.make_async_copy(src.at[0], dst, wsem.at[i])
        for i, (src, dst) in enumerate(((wg_hbm, wg), (wu_hbm, wu), (wd_hbm, wd)))
    ]
    for load in loads:
        load.start()

    barrier = pltpu.get_barrier_semaphore()

    def greet(step, carry):
        pl.semaphore_signal(
            barrier, inc=1, device_id={"ep": lax.rem(me + step, n)},
            device_id_type=pl.DeviceIdType.MESH,
        )
        return carry

    lax.fori_loop(1, n, greet, 0)

    slot_expert = iota((rows, slots), 1) // CAP
    named = jnp.zeros((rows, slots), F32)
    weight = jnp.zeros((rows, slots), F32)
    for k in range(top):
        hit = jnp.where(routes[:, k : k + 1] == slot_expert, 1.0, 0.0)
        named = named + hit
        weight = weight + hit * gates[:, k : k + 1].astype(F32)
    earlier = one_hot(iota((rows, rows), 1) < iota((rows, rows), 0))
    place = mm(earlier, named.astype(BF16))
    copy_of = lax.rem(iota((rows, slots), 1), CAP).astype(F32)
    chosen = jnp.where(place == copy_of, named, 0.0)
    scaled = chosen * weight * (1.0 / 256.0)

    packet_rows = experts * TILE
    spread = one_hot(
        (iota((packet_rows, slots), 0) // TILE * CAP + lax.rem(iota((packet_rows, slots), 0), CAP))
        == iota((packet_rows, slots), 1)
    )
    chosen_all = jnp.concatenate([chosen.astype(BF16)] * blocks, axis=0)
    shape = (packet_rows, blocks * rows)
    in_block = lax.rem(iota(shape, 0), TILE) // CAP == iota(shape, 1) // rows
    pick = jnp.where(in_block, mm_nt(spread, chosen_all), 0.0).astype(BF16)
    for h in range(SPLIT):
        stacked = jnp.concatenate(
            [tokens[:, h * half + b * BLOCK : h * half + (b + 1) * BLOCK] for b in range(blocks)],
            axis=0,
        )
        send[h] = mm(pick, stacked).astype(BF16).reshape(experts, TILE, BLOCK)

    pl.semaphore_wait(barrier, n - 1)

    def outgoing(dest):
        return pltpu.make_async_remote_copy(
            src_ref=send.at[lax.rem(dest, SPLIT), dest // SPLIT], dst_ref=recv.at[me],
            send_sem=send_s.at[dest], recv_sem=send_r.at[me],
            device_id={"ep": dest}, device_id_type=pl.DeviceIdType.MESH,
        )

    def incoming(src):
        return pltpu.make_async_remote_copy(
            src_ref=send.at[0, 0], dst_ref=recv.at[src],
            send_sem=send_s.at[src], recv_sem=send_r.at[src],
            device_id={"ep": src}, device_id_type=pl.DeviceIdType.MESH,
        )

    def relay(src):
        return pltpu.make_async_remote_copy(
            src_ref=recv.at[src], dst_ref=relayed.at[src],
            send_sem=relay_s.at[src], recv_sem=relay_r.at[src],
            device_id={"ep": partner}, device_id_type=pl.DeviceIdType.MESH,
        )

    def send_one(step, carry):
        outgoing(lax.rem(me + step, n)).start()
        return carry

    lax.fori_loop(1, n, send_one, 0)
    recv[me] = send[side, me // SPLIT]
    relay(me).start()

    def pass_on(step, carry):
        src = lax.rem(me + n - step, n)
        incoming(src).wait_recv()
        relay(src).start()
        return carry

    lax.fori_loop(1, n, pass_on, 0)

    shape = (blocks * group * CAP, group * TILE)
    line, col = iota(shape, 0), iota(shape, 1)
    source_row = lax.rem(line, group * CAP)
    gather = one_hot(
        col == source_row // CAP * TILE + line // (group * CAP) * CAP + lax.rem(source_row, CAP)
    )
    shape = shape[::-1]
    line, col = iota(shape, 1), iota(shape, 0)
    source_row = lax.rem(line, group * CAP)
    scatter = one_hot(
        col == source_row // CAP * TILE + line // (group * CAP) * CAP + lax.rem(source_row, CAP)
    )

    def unpack(ref):
        parts = []
        for g in range(n // group):
            flat = ref[g * group : (g + 1) * group].reshape(group * TILE, BLOCK)
            tall = mm(gather, flat).astype(BF16)
            parts.append(
                jnp.concatenate(
                    [tall[b * group * CAP : (b + 1) * group * CAP] for b in range(blocks)], axis=1
                )
            )
        return jnp.concatenate(parts, axis=0) if len(parts) > 1 else parts[0]

    own_rows = pl.ds(pl.multiple_of(side * half, BLOCK // 2), half)
    other_rows = pl.ds(pl.multiple_of((1 - side) * half, BLOCK // 2), half)
    mine = unpack(recv)
    loads[0].wait()
    gate_part = mm(mine, wg[own_rows, :])
    loads[1].wait()
    up_part = mm(mine, wu[own_rows, :])

    def relay_arrived(src, carry):
        relay(src).wait_recv()
        return carry

    lax.fori_loop(0, n, relay_arrived, 0)
    theirs = unpack(relayed)
    gate_part = gate_part + mm(theirs, wg[other_rows, :])
    up_part = up_part + mm(theirs, wu[other_rows, :])
    hidden = (gate_part / (1.0 + jnp.exp(-gate_part)) * up_part).astype(BF16)

    loads[2].wait()
    zsend[...] = mm(hidden, wd[:, other_rows])
    exchange = pltpu.make_async_remote_copy(
        src_ref=zsend, dst_ref=zrecv, send_sem=z_s, recv_sem=z_r,
        device_id={"ep": partner}, device_id_type=pl.DeviceIdType.MESH,
    )
    exchange.start()
    kept = mm(hidden, wd[:, own_rows])
    exchange.wait_recv()
    total = (kept + zrecv[...]).astype(BF16)
    for g in range(n // group):
        lines = slice(g * group * CAP, (g + 1) * group * CAP)
        tall = jnp.concatenate(
            [total[lines, b * BLOCK : (b + 1) * BLOCK] for b in range(blocks)], axis=0
        )
        rsend[g * group : (g + 1) * group] = (
            mm(scatter, tall).astype(BF16).reshape(group, TILE, BLOCK)
        )

    def give_back(dest):
        return pltpu.make_async_remote_copy(
            src_ref=rsend.at[dest], dst_ref=ret.at[side, me // SPLIT],
            send_sem=ret_s.at[dest], recv_sem=ret_r.at[me],
            device_id={"ep": dest}, device_id_type=pl.DeviceIdType.MESH,
        )

    def given(src):
        return pltpu.make_async_remote_copy(
            src_ref=rsend.at[src], dst_ref=ret.at[lax.rem(src, SPLIT), src // SPLIT],
            send_sem=ret_s.at[src], recv_sem=ret_r.at[src],
            device_id={"ep": src}, device_id_type=pl.DeviceIdType.MESH,
        )

    def return_one(step, carry):
        give_back(lax.rem(me + step, n)).start()
        return carry

    lax.fori_loop(1, n, return_one, 0)
    ret[side, me // SPLIT] = rsend[me]

    scaled_all = jnp.concatenate([scaled.astype(BF16)] * blocks, axis=0)
    shape = (blocks * rows, packet_rows)
    in_block = lax.rem(iota(shape, 1), TILE) // CAP == iota(shape, 0) // rows
    mix = jnp.where(in_block, mm_nt(scaled_all, spread), 0.0).astype(BF16)

    def drain(step, carry):
        other = lax.rem(me + step, n)
        outgoing(other).wait_send()
        relay(other).wait_send()
        return carry

    lax.fori_loop(1, n, drain, 0)
    relay(me).wait_send()
    exchange.wait_send()

    def returned(step, carry):
        given(lax.rem(me + n - step, n)).wait_recv()
        return carry

    lax.fori_loop(1, n, returned, 0)
    for h in range(SPLIT):
        tall = mm(mix, ret[h].reshape(packet_rows, BLOCK)).astype(BF16)
        for b in range(blocks):
            out[:, h * half + b * BLOCK : h * half + (b + 1) * BLOCK] = tall[
                b * rows : (b + 1) * rows
            ]

    def drain_back(step, carry):
        give_back(lax.rem(me + step, n)).wait_send()
        return carry

    lax.fori_loop(1, n, drain_back, 0)


def shards(tokens, routes, gate_num, w_gate, w_up, w_down):
    n = lax.axis_size("ep")
    rows, width = tokens.shape
    half = width // SPLIT
    experts = n // SPLIT
    group = min(n, 16)
    vmem = pl.BlockSpec(memory_space=pltpu.VMEM)
    hbm = pl.BlockSpec(memory_space=pl.ANY)
    sems = pltpu.SemaphoreType.DMA
    return pl.pallas_call(
        functools.partial(kernel, n, group),
        out_shape=jax.ShapeDtypeStruct((rows, width), BF16),
        in_specs=[vmem, vmem, vmem, hbm, hbm, hbm],
        out_specs=vmem,
        scratch_shapes=[
            pltpu.VMEM(w_gate.shape[1:], BF16),
            pltpu.VMEM(w_up.shape[1:], BF16),
            pltpu.VMEM(w_down.shape[1:], BF16),
            pltpu.VMEM((SPLIT, experts, TILE, BLOCK), BF16),
            pltpu.VMEM((n, TILE, BLOCK), BF16),
            pltpu.VMEM((n, TILE, BLOCK), BF16),
            pltpu.VMEM((n * CAP, half), F32),
            pltpu.VMEM((n * CAP, half), F32),
            pltpu.VMEM((n, TILE, BLOCK), BF16),
            pltpu.VMEM((SPLIT, experts, TILE, BLOCK), BF16),
            sems((3,)),
            sems((n,)), sems((n,)),
            sems((n,)), sems((n,)),
            sems, sems,
            sems((n,)), sems((n,)),
        ],
        compiler_params=pltpu.CompilerParams(
            collective_id=0, has_side_effects=True, vmem_limit_bytes=56 << 20
        ),
    )(tokens, routes, gate_num, w_gate, w_up, w_down)


def solution(mesh):
    return jax.shard_map(
        shards,
        mesh=mesh,
        in_specs=(
            P(("groups", "ep"), None),
            P(("groups", "ep"), None),
            P(("groups", "ep"), None),
            P("ep", None, None),
            P("ep", None, None),
            P("ep", None, None),
        ),
        out_specs=P(("groups", "ep"), None),
        check_vma=False,
    )
```

```python
import functools

import jax
import jax.numpy as jnp
from jax import lax
from jax.experimental import pallas as pl
from jax.experimental.pallas import tpu as pltpu
from jax.sharding import PartitionSpec as P

SPLIT = 2
CAP = 2
BLOCK = 512
TILE = 16
F32 = jnp.float32
BF16 = jnp.bfloat16
MESH = pl.DeviceIdType.MESH


def iota(shape, dim):
    return lax.broadcasted_iota(jnp.int32, shape, dim)


def over(x, k):
    return x >> (k.bit_length() - 1) if k & (k - 1) == 0 else x // k


def mod(x, k):
    return x & (k - 1) if k & (k - 1) == 0 else x - x // k * k


def mm(a, b):
    return jnp.dot(a, b, preferred_element_type=F32)


def mm_nt(a, b):
    return lax.dot_general(a, b, (((1,), (1,)), ((), ())), preferred_element_type=F32)


def one_hot(cond):
    return jnp.where(cond, 1.0, 0.0).astype(BF16)


def packet_map(shape, group, line_dim):
    line, col = iota(shape, line_dim), iota(shape, 1 - line_dim)
    row = mod(line, group * CAP)
    return one_hot(col == over(row, CAP) * TILE + over(line, group * CAP) * CAP + mod(row, CAP))


def kernel(
    n, group, tokens_hbm, routes_hbm, gates_hbm, wg_hbm, wu_hbm, wd_hbm, ret, mix,
    tokens, routes, gates, wg, wu, wd, send, recv, relayed, kept, zsend, zrecv, rsend, gather, scatter,
    small_s, wsem, send_s, send_r, relay_s, relay_r, z_s, z_r, ret_s, ret_r,
):
    me = lax.axis_index("ep")
    side = lax.rem(me, SPLIT)
    here = me // SPLIT
    partner = me + 1 - 2 * side
    rows, width = tokens.shape
    top = routes.shape[0]
    blocks = width // BLOCK
    chips = n // SPLIT
    slots = chips * CAP
    half_rows = chips * CAP
    tiled_rows = blocks * rows

    barrier = pltpu.get_barrier_semaphore()

    def there(step):
        return lax.rem(here + step, chips)

    def greet(step, carry):
        pl.semaphore_signal(
            barrier, inc=1, device_id={"ep": there(step) * SPLIT + side}, device_id_type=MESH
        )
        return carry

    lax.fori_loop(1, chips, greet, 0)
    pl.semaphore_signal(barrier, inc=1, device_id={"ep": partner}, device_id_type=MESH)

    small = [
        pltpu.make_async_copy(src, dst, small_s.at[i])
        for i, (src, dst) in enumerate(
            ((routes_hbm, routes), (gates_hbm, gates), (tokens_hbm, tokens))
        )
    ]
    loads = [
        pltpu.make_async_copy(src.at[0], dst, wsem.at[i])
        for i, (src, dst) in enumerate(((wg_hbm, wg), (wu_hbm, wu), (wd_hbm, wd)))
    ]
    for load in small + loads:
        load.start()

    shape = (rows, tiled_rows)
    token_of = mod(iota(shape, 1), rows)
    repeat = one_hot(token_of == iota(shape, 0))
    earlier = one_hot(iota(shape, 0) < token_of)
    packet_rows = chips * TILE
    shape = (packet_rows, slots)
    line = iota(shape, 0)
    spread = one_hot(over(line, TILE) * CAP + mod(line, CAP) == iota(shape, 1))
    shape = (packet_rows, tiled_rows)
    in_block = over(mod(iota(shape, 0), TILE), CAP) == over(iota(shape, 1), rows)
    shape = (slots, tiled_rows)
    expert_of = over(iota(shape, 0), CAP).astype(F32)
    copy_of = mod(iota(shape, 0), CAP).astype(F32)
    small[0].wait()
    small[1].wait()
    ints = jnp.concatenate([routes[...], gates[...]], axis=0).astype(F32).astype(BF16)
    tiled = mm(ints, repeat)
    named = jnp.zeros(shape, F32)
    weight = jnp.zeros(shape, F32)
    for k in range(top):
        hit = tiled[k : k + 1] == expert_of
        named = jnp.where(hit, 1.0, named)
        weight = jnp.where(hit, tiled[top + k : top + k + 1], weight)
    place = mm(named[:, :rows].astype(BF16), earlier)
    chosen = jnp.where(place == copy_of, named, 0.0)

    pick = jnp.where(in_block, mm(spread, chosen.astype(BF16)), 0.0).astype(BF16)
    small[2].wait()
    stacked = jnp.concatenate(
        [tokens[:, b * BLOCK : (b + 1) * BLOCK] for b in range(blocks)], axis=0
    )
    send[...] = mm(pick, stacked).astype(BF16).reshape(chips, TILE, BLOCK)

    pl.semaphore_wait(barrier, chips)

    def outgoing(q):
        return pltpu.make_async_remote_copy(
            src_ref=send.at[q], dst_ref=recv.at[here], send_sem=send_s.at[q],
            recv_sem=send_r.at[here], device_id={"ep": q * SPLIT + side}, device_id_type=MESH,
        )

    def incoming(q):
        return pltpu.make_async_remote_copy(
            src_ref=send.at[q], dst_ref=recv.at[q], send_sem=send_s.at[q],
            recv_sem=send_r.at[q], device_id={"ep": q * SPLIT + side}, device_id_type=MESH,
        )

    def relay(q):
        return pltpu.make_async_remote_copy(
            src_ref=recv.at[q], dst_ref=relayed.at[q], send_sem=relay_s.at[q],
            recv_sem=relay_r.at[q], device_id={"ep": partner}, device_id_type=MESH,
        )

    def send_one(step, carry):
        outgoing(there(step)).start()
        return carry

    lax.fori_loop(1, chips, send_one, 0)
    recv[here] = send[here]
    relay(here).start()

    gather[...] = packet_map((blocks * group * CAP, group * TILE), group, 0)
    scatter[...] = packet_map((group * TILE, blocks * group * CAP), group, 1)
    scaled = (chosen * weight * (1.0 / 256.0)).astype(BF16)
    pick_scaled = jnp.where(in_block, mm(spread, scaled), 0.0).astype(BF16)
    shape = (tiled_rows, tiled_rows)
    mix[...] = mm_nt(one_hot(iota(shape, 0) == iota(shape, 1)), pick_scaled).astype(BF16)

    def pass_on(step, carry):
        q = there(chips - step)
        incoming(q).wait_recv()
        relay(q).start()
        return carry

    lax.fori_loop(1, chips, pass_on, 0)

    def unpack(ref):
        parts = []
        for g in range(chips // group):
            flat = ref[g * group : (g + 1) * group].reshape(group * TILE, BLOCK)
            tall = mm(gather[...], flat).astype(BF16)
            step = group * CAP
            parts.append(
                jnp.concatenate([tall[b * step : (b + 1) * step] for b in range(blocks)], axis=1)
            )
        return parts

    mine = unpack(recv)
    loads[0].wait()
    loads[1].wait()

    def relay_arrived(step, carry):
        relay(there(step)).wait_recv()
        return carry

    lax.fori_loop(0, chips, relay_arrived, 0)
    x = jnp.concatenate(mine + unpack(relayed), axis=0)
    gate_part = mm(x, wg[...])
    up_part = mm(x, wu[...])
    hidden = (gate_part / (1.0 + jnp.exp(-gate_part)) * up_part).astype(BF16)

    def exchange(b):
        return pltpu.make_async_remote_copy(
            src_ref=zsend.at[b], dst_ref=zrecv.at[b], send_sem=z_s.at[b], recv_sem=z_r.at[b],
            device_id={"ep": partner}, device_id_type=MESH,
        )

    loads[2].wait()
    for b in range(blocks):
        z = mm(hidden, wd[:, b * BLOCK : (b + 1) * BLOCK])
        zsend[b] = z[half_rows:]
        exchange(b).start()
        kept[b] = z[:half_rows]
    total = []
    for b in range(blocks):
        exchange(b).wait_recv()
        total.append((kept[b] + zrecv[b]).astype(BF16))
    for g in range(chips // group):
        lines = slice(g * group * CAP, (g + 1) * group * CAP)
        tall = jnp.concatenate([part[lines] for part in total], axis=0)
        packed = mm(scatter[...], tall).astype(BF16)
        rsend[g * group : (g + 1) * group] = packed.reshape(group, TILE, BLOCK)

    def give_back(q):
        return pltpu.make_async_remote_copy(
            src_ref=rsend.at[q], dst_ref=ret.at[here], send_sem=ret_s.at[q],
            recv_sem=ret_r.at[here], device_id={"ep": q * SPLIT + side}, device_id_type=MESH,
        )

    def given(q):
        return pltpu.make_async_remote_copy(
            src_ref=rsend.at[q], dst_ref=ret.at[q], send_sem=ret_s.at[q],
            recv_sem=ret_r.at[q], device_id={"ep": q * SPLIT + side}, device_id_type=MESH,
        )

    def return_one(step, carry):
        give_back(there(step)).start()
        return carry

    lax.fori_loop(1, chips, return_one, 0)
    ret[here] = rsend[here]

    def drain(step, carry):
        outgoing(there(step)).wait_send()
        relay(there(step)).wait_send()
        return carry

    lax.fori_loop(1, chips, drain, 0)
    relay(here).wait_send()
    for b in range(blocks):
        exchange(b).wait_send()

    def returned(step, carry):
        given(there(chips - step)).wait_recv()
        return carry

    lax.fori_loop(1, chips, returned, 0)

    def drain_back(step, carry):
        give_back(there(step)).wait_send()
        return carry

    lax.fori_loop(1, chips, drain_back, 0)


def combine(ret, mix, out):
    rows = out.shape[0]
    chips = ret.shape[0]
    tall = mm(mix[...], ret[...].reshape(chips * TILE, BLOCK)).astype(BF16)
    for b in range(out.shape[1] // BLOCK):
        out[:, b * BLOCK : (b + 1) * BLOCK] = tall[b * rows : (b + 1) * rows]


def shards(tokens, routes, gate_num, w_gate, w_up, w_down):
    n = lax.axis_size("ep")
    rows, width = tokens.shape
    top = routes.shape[1]
    chips = n // SPLIT
    blocks = width // BLOCK
    group = min(chips, 8)
    half_rows = chips * CAP
    vmem = pl.BlockSpec(memory_space=pltpu.VMEM)
    hbm = pl.BlockSpec(memory_space=pl.ANY)
    sems = pltpu.SemaphoreType.DMA
    ret, mix = pl.pallas_call(
        functools.partial(kernel, n, group),
        out_shape=[
            jax.ShapeDtypeStruct((chips, TILE, BLOCK), BF16),
            jax.ShapeDtypeStruct((blocks * rows, chips * TILE), BF16),
        ],
        in_specs=[hbm] * 6,
        out_specs=[vmem, vmem],
        scratch_shapes=[
            pltpu.VMEM((rows, width), BF16),
            pltpu.VMEM((top, rows), jnp.int32),
            pltpu.VMEM((top, rows), jnp.int32),
            pltpu.VMEM(w_gate.shape[1:], BF16),
            pltpu.VMEM(w_up.shape[1:], BF16),
            pltpu.VMEM(w_down.shape[1:], BF16),
            pltpu.VMEM((chips, TILE, BLOCK), BF16),
            pltpu.VMEM((chips, TILE, BLOCK), BF16),
            pltpu.VMEM((chips, TILE, BLOCK), BF16),
            pltpu.VMEM((blocks, half_rows, BLOCK), F32),
            pltpu.VMEM((blocks, half_rows, BLOCK), F32),
            pltpu.VMEM((blocks, half_rows, BLOCK), F32),
            pltpu.VMEM((chips, TILE, BLOCK), BF16),
            pltpu.VMEM((blocks * group * CAP, group * TILE), BF16),
            pltpu.VMEM((group * TILE, blocks * group * CAP), BF16),
            sems((3,)),
            sems((3,)),
            sems((chips,)), sems((chips,)),
            sems((chips,)), sems((chips,)),
            sems((blocks,)), sems((blocks,)),
            sems((chips,)), sems((chips,)),
        ],
        compiler_params=pltpu.CompilerParams(
            collective_id=0, has_side_effects=True, vmem_limit_bytes=56 << 20
        ),
    )(tokens, routes.T, gate_num.T, w_gate, w_up, w_down)
    return pl.pallas_call(
        combine,
        out_shape=jax.ShapeDtypeStruct((rows, width), BF16),
        in_specs=[vmem, vmem],
        out_specs=vmem,
    )(ret, mix)


def solution(mesh):
    return jax.shard_map(
        shards,
        mesh=mesh,
        in_specs=(
            P(("groups", "ep"), None),
            P(("groups", "ep"), None),
            P(("groups", "ep"), None),
            P("ep", None, None),
            P("ep", None, None),
            P("ep", None, None),
        ),
        out_specs=P(("groups", "ep"), None),
        check_vma=False,
    )
```

```python
import functools

import jax
import jax.numpy as jnp
from jax import lax
from jax.experimental import pallas as pl
from jax.experimental.pallas import tpu as pltpu
from jax.sharding import PartitionSpec as P

SPLIT = 2
CAP = 2
BLOCK = 256
PARTS = 2
TILE = 16
F32 = jnp.float32
BF16 = jnp.bfloat16
MESH = pl.DeviceIdType.MESH


def iota(shape, dim):
    return lax.broadcasted_iota(jnp.int32, shape, dim)


def over(x, k):
    return x >> (k.bit_length() - 1) if k & (k - 1) == 0 else x // k


def mod(x, k):
    return x & (k - 1) if k & (k - 1) == 0 else x - x // k * k


def mm(a, b):
    return jnp.dot(a, b, preferred_element_type=F32)


def mm_nt(a, b):
    return lax.dot_general(a, b, (((1,), (1,)), ((), ())), preferred_element_type=F32)


def one_hot(cond):
    return jnp.where(cond, 1.0, 0.0).astype(BF16)


def packet_map(shape, group, line_dim):
    line, col = iota(shape, line_dim), iota(shape, 1 - line_dim)
    row = mod(line, group * CAP)
    return one_hot(col == over(row, CAP) * TILE + over(line, group * CAP) * CAP + mod(row, CAP))


def kernel(
    n, group, tokens, routes, gates, wg_hbm, wu_hbm, wd_hbm, ret, mix,
    wg, wu, wd, send, recv, relayed, kept, zsend, zrecv, rsend, gather, scatter, wsem, send_s, send_r, relay_s, relay_r, z_s, z_r, ret_s, ret_r,
):
    me = lax.axis_index("ep")
    side = lax.rem(me, SPLIT)
    here = me // SPLIT
    partner = me + 1 - 2 * side
    rows, width = tokens.shape
    top = routes.shape[0]
    part = width // PARTS
    blocks = part // BLOCK
    chips = n // SPLIT
    slots = chips * CAP
    half_rows = chips * CAP
    tiled_rows = blocks * rows

    barrier = pltpu.get_barrier_semaphore()

    middle = chips // 2
    base = here // middle * middle

    def others(act, back=False):
        def across(step, carry):
            act(middle - base + lax.rem(here + (middle - step if back else step), middle))
            return carry

        def beside(step, carry):
            act(base + lax.rem(here + (middle - step if back else step), middle))
            return carry

        lax.fori_loop(0, middle, across, 0)
        lax.fori_loop(1, middle, beside, 0)

    def greet(q):
        pl.semaphore_signal(
            barrier, inc=1, device_id={"ep": q * SPLIT + side}, device_id_type=MESH
        )

    others(greet)
    pl.semaphore_signal(barrier, inc=1, device_id={"ep": partner}, device_id_type=MESH)

    loads = [
        pltpu.make_async_copy(src.at[0], dst, wsem.at[i])
        for i, (src, dst) in enumerate(((wg_hbm, wg), (wu_hbm, wu), (wd_hbm, wd)))
    ]
    for load in loads:
        load.start()

    shape = (rows, tiled_rows)
    token_of = mod(iota(shape, 1), rows)
    repeat = one_hot(token_of == iota(shape, 0))
    earlier = one_hot(iota(shape, 0) < token_of)
    packet_rows = chips * TILE
    shape = (packet_rows, slots)
    line = iota(shape, 0)
    spread = one_hot(over(line, TILE) * CAP + mod(line, CAP) == iota(shape, 1))
    shape = (packet_rows, tiled_rows)
    in_block = over(mod(iota(shape, 0), TILE), CAP) == over(iota(shape, 1), rows)
    shape = (slots, tiled_rows)
    expert_of = over(iota(shape, 0), CAP).astype(F32)
    copy_of = mod(iota(shape, 0), CAP).astype(F32)
    ints = jnp.concatenate([routes[...], gates[...]], axis=0).astype(F32).astype(BF16)
    tiled = mm(ints, repeat)
    named = jnp.zeros(shape, F32)
    weight = jnp.zeros(shape, F32)
    for k in range(top):
        hit = tiled[k : k + 1] == expert_of
        named = jnp.where(hit, 1.0, named)
        weight = jnp.where(hit, tiled[top + k : top + k + 1], weight)
    place = mm(named[:, :rows].astype(BF16), earlier)
    chosen = jnp.where(place == copy_of, named, 0.0)

    pick = jnp.where(in_block, mm(spread, chosen.astype(BF16)), 0.0).astype(BF16)

    def outgoing(h, q):
        return pltpu.make_async_remote_copy(
            src_ref=send.at[h, q], dst_ref=recv.at[h, here], send_sem=send_s.at[h, q],
            recv_sem=send_r.at[h, here], device_id={"ep": q * SPLIT + side}, device_id_type=MESH,
        )

    def incoming(h, q):
        return pltpu.make_async_remote_copy(
            src_ref=send.at[h, q], dst_ref=recv.at[h, q], send_sem=send_s.at[h, q],
            recv_sem=send_r.at[h, q], device_id={"ep": q * SPLIT + side}, device_id_type=MESH,
        )

    def relay(h, q):
        return pltpu.make_async_remote_copy(
            src_ref=recv.at[h, q], dst_ref=relayed.at[h, q], send_sem=relay_s.at[h, q],
            recv_sem=relay_r.at[h, q], device_id={"ep": partner}, device_id_type=MESH,
        )

    for h in range(PARTS):
        stacked = jnp.concatenate(
            [tokens[:, h * part + b * BLOCK : h * part + (b + 1) * BLOCK] for b in range(blocks)],
            axis=0,
        )
        send[h] = mm(pick, stacked).astype(BF16).reshape(chips, TILE, BLOCK)
        if h == 0:
            pl.semaphore_wait(barrier, chips)
        others(lambda q: outgoing(h, q).start())
    for h in range(PARTS):
        recv[h, here] = send[h, here]
        relay(h, here).start()

    gather[...] = packet_map((blocks * group * CAP, group * TILE), group, 0)
    scatter[...] = packet_map((group * TILE, blocks * group * CAP), group, 1)
    scaled = (chosen * weight * (1.0 / 256.0)).astype(BF16)
    pick_scaled = jnp.where(in_block, mm(spread, scaled), 0.0).astype(BF16)
    shape = (tiled_rows, tiled_rows)
    mix[...] = mm_nt(one_hot(iota(shape, 0) == iota(shape, 1)), pick_scaled).astype(BF16)

    def unpack(ref, h):
        parts = []
        step = group * CAP
        for g in range(chips // group):
            flat = ref[h, g * group : (g + 1) * group].reshape(group * TILE, BLOCK)
            tall = mm(gather[...], flat).astype(BF16)
            parts.append(
                jnp.concatenate([tall[b * step : (b + 1) * step] for b in range(blocks)], axis=1)
            )
        return parts

    for h in range(PARTS):

        def pass_on(q):
            incoming(h, q).wait_recv()
            relay(h, q).start()

        others(pass_on, back=True)

    loads[0].wait()
    loads[1].wait()
    gate_part = up_part = None
    for h in range(PARTS):
        relay(h, here).wait_recv()
        others(lambda q: relay(h, q).wait_recv(), back=True)
        x = jnp.concatenate(unpack(recv, h) + unpack(relayed, h), axis=0)
        gate_more = mm(x, wg[h * part : (h + 1) * part])
        up_more = mm(x, wu[h * part : (h + 1) * part])
        gate_part = gate_more if h == 0 else gate_part + gate_more
        up_part = up_more if h == 0 else up_part + up_more
    hidden = (gate_part / (1.0 + jnp.exp(-gate_part)) * up_part).astype(BF16)

    def exchange(h):
        return pltpu.make_async_remote_copy(
            src_ref=zsend.at[h], dst_ref=zrecv.at[h], send_sem=z_s.at[h], recv_sem=z_r.at[h],
            device_id={"ep": partner}, device_id_type=MESH,
        )

    def give_back(h, q):
        return pltpu.make_async_remote_copy(
            src_ref=rsend.at[h, q], dst_ref=ret.at[h, here], send_sem=ret_s.at[h, q],
            recv_sem=ret_r.at[h, here], device_id={"ep": q * SPLIT + side}, device_id_type=MESH,
        )

    def given(h, q):
        return pltpu.make_async_remote_copy(
            src_ref=rsend.at[h, q], dst_ref=ret.at[h, q], send_sem=ret_s.at[h, q],
            recv_sem=ret_r.at[h, q], device_id={"ep": q * SPLIT + side}, device_id_type=MESH,
        )

    loads[2].wait()
    for h in range(PARTS):
        z = mm(hidden, wd[:, h * part : (h + 1) * part])
        zsend[h] = z[half_rows:]
        exchange(h).start()
        kept[h] = z[:half_rows]
    for h in range(PARTS):
        exchange(h).wait_recv()
        total = (kept[h] + zrecv[h]).astype(BF16)
        for g in range(chips // group):
            lines = slice(g * group * CAP, (g + 1) * group * CAP)
            tall = jnp.concatenate(
                [total[lines, b * BLOCK : (b + 1) * BLOCK] for b in range(blocks)], axis=0
            )
            packed = mm(scatter[...], tall).astype(BF16)
            rsend[h, g * group : (g + 1) * group] = packed.reshape(group, TILE, BLOCK)
        others(lambda q: give_back(h, q).start())
        ret[h, here] = rsend[h, here]

    for h in range(PARTS):

        def sent(q):
            outgoing(h, q).wait_send()
            relay(h, q).wait_send()

        others(sent)
        relay(h, here).wait_send()
        exchange(h).wait_send()
    for h in range(PARTS):
        others(lambda q: given(h, q).wait_recv(), back=True)
    for h in range(PARTS):
        others(lambda q: give_back(h, q).wait_send())


def combine(ret, mix, out):
    rows = out.shape[0]
    chips = ret.shape[1]
    part = out.shape[1] // PARTS
    for h in range(PARTS):
        tall = mm(mix[...], ret[h].reshape(chips * TILE, BLOCK)).astype(BF16)
        for b in range(part // BLOCK):
            at = h * part + b * BLOCK
            out[:, at : at + BLOCK] = tall[b * rows : (b + 1) * rows]


def shards(tokens, routes, gate_num, w_gate, w_up, w_down):
    n = lax.axis_size("ep")
    rows, width = tokens.shape
    chips = n // SPLIT
    part = width // PARTS
    blocks = part // BLOCK
    group = min(chips, 8)
    half_rows = chips * CAP
    vmem = pl.BlockSpec(memory_space=pltpu.VMEM)
    hbm = pl.BlockSpec(memory_space=pltpu.HBM)
    sems = pltpu.SemaphoreType.DMA
    ret, mix = pl.pallas_call(
        functools.partial(kernel, n, group),
        out_shape=[
            jax.ShapeDtypeStruct((PARTS, chips, TILE, BLOCK), BF16),
            jax.ShapeDtypeStruct((blocks * rows, chips * TILE), BF16),
        ],
        in_specs=[vmem] * 3 + [hbm] * 3,
        out_specs=[vmem, vmem],
        scratch_shapes=[
            pltpu.VMEM(w_gate.shape[1:], BF16),
            pltpu.VMEM(w_up.shape[1:], BF16),
            pltpu.VMEM(w_down.shape[1:], BF16),
            pltpu.VMEM((PARTS, chips, TILE, BLOCK), BF16),
            pltpu.VMEM((PARTS, chips, TILE, BLOCK), BF16),
            pltpu.VMEM((PARTS, chips, TILE, BLOCK), BF16),
            pltpu.VMEM((PARTS, half_rows, part), F32),
            pltpu.VMEM((PARTS, half_rows, part), F32),
            pltpu.VMEM((PARTS, half_rows, part), F32),
            pltpu.VMEM((PARTS, chips, TILE, BLOCK), BF16),
            pltpu.VMEM((blocks * group * CAP, group * TILE), BF16),
            pltpu.VMEM((group * TILE, blocks * group * CAP), BF16),
            sems((3,)),
            sems((PARTS, chips)), sems((PARTS, chips)),
            sems((PARTS, chips)), sems((PARTS, chips)),
            sems((PARTS,)), sems((PARTS,)),
            sems((PARTS, chips)), sems((PARTS, chips)),
        ],
        compiler_params=pltpu.CompilerParams(
            collective_id=0, has_side_effects=True, vmem_limit_bytes=52 << 20
        ),
    )(tokens, routes.T, gate_num.T, w_gate, w_up, w_down)
    return pl.pallas_call(
        combine,
        out_shape=jax.ShapeDtypeStruct((rows, width), BF16),
        in_specs=[vmem, vmem],
        out_specs=vmem,
    )(ret, mix)


def solution(mesh):
    return jax.shard_map(
        shards,
        mesh=mesh,
        in_specs=(
            P(("groups", "ep"), None),
            P(("groups", "ep"), None),
            P(("groups", "ep"), None),
            P("ep", None, None),
            P("ep", None, None),
            P("ep", None, None),
        ),
        out_specs=P(("groups", "ep"), None),
        check_vma=False,
    )
```

```python
import functools

import jax
import jax.numpy as jnp
from jax import lax
from jax.experimental import pallas as pl
from jax.experimental.pallas import tpu as pltpu
from jax.sharding import PartitionSpec as P

SPLIT = 2
CAP = 2
BLOCK = 256
PARTS = 2
TILE = 16
F32 = jnp.float32
BF16 = jnp.bfloat16
MESH = pl.DeviceIdType.MESH


def iota(shape, dim):
    return lax.broadcasted_iota(jnp.int32, shape, dim)


def over(x, k):
    return x >> (k.bit_length() - 1) if k & (k - 1) == 0 else x // k


def mod(x, k):
    return x & (k - 1) if k & (k - 1) == 0 else x - x // k * k


def mm(a, b):
    return jnp.dot(a, b, preferred_element_type=F32)


def mm_nt(a, b):
    return lax.dot_general(a, b, (((1,), (1,)), ((), ())), preferred_element_type=F32)


def one_hot(cond):
    return jnp.where(cond, 1.0, 0.0).astype(BF16)


def packet_map(shape, group, line_dim):
    line, col = iota(shape, line_dim), iota(shape, 1 - line_dim)
    row = mod(line, group * CAP)
    return one_hot(col == over(row, CAP) * TILE + over(line, group * CAP) * CAP + mod(row, CAP))


def kernel(
    n, group, tokens_hbm, routes, gates, wg_hbm, wu_hbm, wd_hbm, out,
    tokens, wg, wu, wd, send, recv, relayed, kept, zsend, zrecv, rsend, ret, gather, scatter,
    mix, rows_s, wsem, send_s, send_r, relay_s, relay_r, z_s, z_r, ret_s, ret_r,
):
    me = lax.axis_index("ep")
    side = lax.rem(me, SPLIT)
    here = me // SPLIT
    partner = me + 1 - 2 * side
    rows, width = tokens.shape
    top = routes.shape[0]
    part = width // PARTS
    blocks = part // BLOCK
    chips = n // SPLIT
    slots = chips * CAP
    half_rows = chips * CAP
    tiled_rows = blocks * rows

    barrier = pltpu.get_barrier_semaphore()

    middle = chips // 2
    base = here // middle * middle

    def others(act, back=False):
        def across(step, carry):
            act(middle - base + lax.rem(here + (middle - step if back else step), middle))
            return carry

        def beside(step, carry):
            act(base + lax.rem(here + (middle - step if back else step), middle))
            return carry

        lax.fori_loop(0, middle, across, 0)
        lax.fori_loop(1, middle, beside, 0)

    def greet(q):
        pl.semaphore_signal(
            barrier, inc=1, device_id={"ep": q * SPLIT + side}, device_id_type=MESH
        )

    others(greet)
    pl.semaphore_signal(barrier, inc=1, device_id={"ep": partner}, device_id_type=MESH)

    fetch = pltpu.make_async_copy(tokens_hbm, tokens, rows_s)
    loads = [
        pltpu.make_async_copy(src.at[0], dst, wsem.at[i])
        for i, (src, dst) in enumerate(((wg_hbm, wg), (wu_hbm, wu), (wd_hbm, wd)))
    ]
    for load in [fetch] + loads:
        load.start()

    shape = (rows, tiled_rows)
    token_of = mod(iota(shape, 1), rows)
    repeat = one_hot(token_of == iota(shape, 0))
    earlier = one_hot(iota(shape, 0) < token_of)
    packet_rows = chips * TILE
    shape = (packet_rows, slots)
    line = iota(shape, 0)
    spread = one_hot(over(line, TILE) * CAP + mod(line, CAP) == iota(shape, 1))
    shape = (packet_rows, tiled_rows)
    in_block = over(mod(iota(shape, 0), TILE), CAP) == over(iota(shape, 1), rows)
    shape = (slots, tiled_rows)
    expert_of = over(iota(shape, 0), CAP).astype(F32)
    copy_of = mod(iota(shape, 0), CAP).astype(F32)
    ints = jnp.concatenate([routes[...], gates[...]], axis=0).astype(F32).astype(BF16)
    tiled = mm(ints, repeat)
    named = jnp.zeros(shape, F32)
    weight = jnp.zeros(shape, F32)
    for k in range(top):
        hit = tiled[k : k + 1] == expert_of
        named = jnp.where(hit, 1.0, named)
        weight = jnp.where(hit, tiled[top + k : top + k + 1], weight)
    place = mm(named[:, :rows].astype(BF16), earlier)
    chosen = jnp.where(place == copy_of, named, 0.0)

    pick = jnp.where(in_block, mm(spread, chosen.astype(BF16)), 0.0).astype(BF16)

    def outgoing(h, q):
        return pltpu.make_async_remote_copy(
            src_ref=send.at[h, q], dst_ref=recv.at[h, here], send_sem=send_s.at[h, q],
            recv_sem=send_r.at[h, here], device_id={"ep": q * SPLIT + side}, device_id_type=MESH,
        )

    def incoming(h, q):
        return pltpu.make_async_remote_copy(
            src_ref=send.at[h, q], dst_ref=recv.at[h, q], send_sem=send_s.at[h, q],
            recv_sem=send_r.at[h, q], device_id={"ep": q * SPLIT + side}, device_id_type=MESH,
        )

    def relay(h, q):
        return pltpu.make_async_remote_copy(
            src_ref=recv.at[h, q], dst_ref=relayed.at[h, q], send_sem=relay_s.at[h, q],
            recv_sem=relay_r.at[h, q], device_id={"ep": partner}, device_id_type=MESH,
        )

    fetch.wait()
    for h in range(PARTS):
        stacked = jnp.concatenate(
            [tokens[:, h * part + b * BLOCK : h * part + (b + 1) * BLOCK] for b in range(blocks)],
            axis=0,
        )
        send[h] = mm(pick, stacked).astype(BF16).reshape(chips, TILE, BLOCK)
        if h == 0:
            pl.semaphore_wait(barrier, chips)
        others(lambda q: outgoing(h, q).start())
    for h in range(PARTS):
        recv[h, here] = send[h, here]
        relay(h, here).start()

    gather[...] = packet_map((blocks * group * CAP, group * TILE), group, 0)
    scatter[...] = packet_map((group * TILE, blocks * group * CAP), group, 1)
    scaled = (chosen * weight * (1.0 / 256.0)).astype(BF16)
    pick_scaled = jnp.where(in_block, mm(spread, scaled), 0.0).astype(BF16)
    shape = (tiled_rows, tiled_rows)
    mix[...] = mm_nt(one_hot(iota(shape, 0) == iota(shape, 1)), pick_scaled).astype(BF16)

    def unpack(ref, h):
        parts = []
        step = group * CAP
        for g in range(chips // group):
            flat = ref[h, g * group : (g + 1) * group].reshape(group * TILE, BLOCK)
            tall = mm(gather[...], flat).astype(BF16)
            parts.append(
                jnp.concatenate([tall[b * step : (b + 1) * step] for b in range(blocks)], axis=1)
            )
        return parts

    for h in range(PARTS):

        def pass_on(q):
            incoming(h, q).wait_recv()
            relay(h, q).start()

        others(pass_on, back=True)

    loads[0].wait()
    loads[1].wait()
    gate_part = up_part = None
    for h in range(PARTS):
        relay(h, here).wait_recv()
        others(lambda q: relay(h, q).wait_recv(), back=True)
        x = jnp.concatenate(unpack(recv, h) + unpack(relayed, h), axis=0)
        gate_more = mm(x, wg[h * part : (h + 1) * part])
        up_more = mm(x, wu[h * part : (h + 1) * part])
        gate_part = gate_more if h == 0 else gate_part + gate_more
        up_part = up_more if h == 0 else up_part + up_more
    hidden = (gate_part / (1.0 + jnp.exp(-gate_part)) * up_part).astype(BF16)

    def exchange(h):
        return pltpu.make_async_remote_copy(
            src_ref=zsend.at[h], dst_ref=zrecv.at[h], send_sem=z_s.at[h], recv_sem=z_r.at[h],
            device_id={"ep": partner}, device_id_type=MESH,
        )

    def give_back(h, q):
        return pltpu.make_async_remote_copy(
            src_ref=rsend.at[h, q], dst_ref=ret.at[h, here], send_sem=ret_s.at[h, q],
            recv_sem=ret_r.at[h, here], device_id={"ep": q * SPLIT + side}, device_id_type=MESH,
        )

    def given(h, q):
        return pltpu.make_async_remote_copy(
            src_ref=rsend.at[h, q], dst_ref=ret.at[h, q], send_sem=ret_s.at[h, q],
            recv_sem=ret_r.at[h, q], device_id={"ep": q * SPLIT + side}, device_id_type=MESH,
        )

    loads[2].wait()
    for h in range(PARTS):
        z = mm(hidden, wd[:, h * part : (h + 1) * part])
        zsend[h] = z[half_rows:]
        exchange(h).start()
        kept[h] = z[:half_rows]
    for h in range(PARTS):
        exchange(h).wait_recv()
        total = (kept[h] + zrecv[h]).astype(BF16)
        for g in range(chips // group):
            lines = slice(g * group * CAP, (g + 1) * group * CAP)
            tall = jnp.concatenate(
                [total[lines, b * BLOCK : (b + 1) * BLOCK] for b in range(blocks)], axis=0
            )
            packed = mm(scatter[...], tall).astype(BF16)
            rsend[h, g * group : (g + 1) * group] = packed.reshape(group, TILE, BLOCK)
        others(lambda q: give_back(h, q).start())
        ret[h, here] = rsend[h, here]

    for h in range(PARTS):

        def sent(q):
            outgoing(h, q).wait_send()
            relay(h, q).wait_send()

        others(sent)
        relay(h, here).wait_send()
        exchange(h).wait_send()
    for h in range(PARTS):
        others(lambda q: given(h, q).wait_recv(), back=True)
        tall = mm(mix[...], ret[h].reshape(packet_rows, BLOCK)).astype(BF16)
        for b in range(blocks):
            at = h * part + b * BLOCK
            out[:, at : at + BLOCK] = tall[b * rows : (b + 1) * rows]
    for h in range(PARTS):
        others(lambda q: give_back(h, q).wait_send())


def shards(tokens, routes, gate_num, w_gate, w_up, w_down):
    n = lax.axis_size("ep")
    rows, width = tokens.shape
    chips = n // SPLIT
    part = width // PARTS
    blocks = part // BLOCK
    group = min(chips, 8)
    half_rows = chips * CAP
    vmem = pl.BlockSpec(memory_space=pltpu.VMEM)
    hbm = pl.BlockSpec(memory_space=pl.ANY)
    sems = pltpu.SemaphoreType.DMA
    return pl.pallas_call(
        functools.partial(kernel, n, group),
        out_shape=jax.ShapeDtypeStruct((rows, width), BF16),
        in_specs=[hbm, vmem, vmem, hbm, hbm, hbm],
        out_specs=vmem,
        scratch_shapes=[
            pltpu.VMEM((rows, width), BF16),
            pltpu.VMEM(w_gate.shape[1:], BF16),
            pltpu.VMEM(w_up.shape[1:], BF16),
            pltpu.VMEM(w_down.shape[1:], BF16),
            pltpu.VMEM((PARTS, chips, TILE, BLOCK), BF16),
            pltpu.VMEM((PARTS, chips, TILE, BLOCK), BF16),
            pltpu.VMEM((PARTS, chips, TILE, BLOCK), BF16),
            pltpu.VMEM((PARTS, half_rows, part), F32),
            pltpu.VMEM((PARTS, half_rows, part), F32),
            pltpu.VMEM((PARTS, half_rows, part), F32),
            pltpu.VMEM((PARTS, chips, TILE, BLOCK), BF16),
            pltpu.VMEM((PARTS, chips, TILE, BLOCK), BF16),
            pltpu.VMEM((blocks * group * CAP, group * TILE), BF16),
            pltpu.VMEM((group * TILE, blocks * group * CAP), BF16),
            pltpu.VMEM((blocks * rows, chips * TILE), BF16),
            sems,
            sems((3,)),
            sems((PARTS, chips)), sems((PARTS, chips)),
            sems((PARTS, chips)), sems((PARTS, chips)),
            sems((PARTS,)), sems((PARTS,)),
            sems((PARTS, chips)), sems((PARTS, chips)),
        ],
        compiler_params=pltpu.CompilerParams(
            collective_id=0, has_side_effects=True, vmem_limit_bytes=54800 << 10
        ),
    )(tokens, routes.T, gate_num.T, w_gate, w_up, w_down)

def solution(mesh):
    return jax.shard_map(
        shards,
        mesh=mesh,
        in_specs=(
            P(("groups", "ep"), None),
            P(("groups", "ep"), None),
            P(("groups", "ep"), None),
            P("ep", None, None),
            P("ep", None, None),
            P("ep", None, None),
        ),
        out_specs=P(("groups", "ep"), None),
        check_vma=False,
    )
```

```python
import functools

import jax
import jax.numpy as jnp
from jax import lax
from jax.experimental import pallas as pl
from jax.experimental.pallas import tpu as pltpu
from jax.sharding import PartitionSpec as P

SPLIT = 2
CAP = 2
BLOCK = 256
PARTS = 2
TILE = 16
F32 = jnp.float32
BF16 = jnp.bfloat16
MESH = pl.DeviceIdType.MESH


def iota(shape, dim):
    return lax.broadcasted_iota(jnp.int32, shape, dim)


def over(x, k):
    return x >> (k.bit_length() - 1) if k & (k - 1) == 0 else x // k


def mod(x, k):
    return x & (k - 1) if k & (k - 1) == 0 else x - x // k * k


def mm(a, b):
    return jnp.dot(a, b, preferred_element_type=F32)


def mm_nt(a, b):
    return lax.dot_general(a, b, (((1,), (1,)), ((), ())), preferred_element_type=F32)


def one_hot(cond):
    return jnp.where(cond, 1.0, 0.0).astype(BF16)


def packet_map(shape, group, line_dim):
    line, col = iota(shape, line_dim), iota(shape, 1 - line_dim)
    row = mod(line, group * CAP)
    return one_hot(col == over(row, CAP) * TILE + over(line, group * CAP) * CAP + mod(row, CAP))


def kernel(
    n, group, tokens_hbm, codes, wg_hbm, wu_hbm, wd_hbm, out,
    tokens, wg, wu, wd, send, recv, relayed, kept, zsend, zrecv, rsend, ret, gather, scatter,
    mix, rows_s, wsem, send_s, send_r, relay_s, relay_r, z_s, z_r, ret_s, ret_r,
):
    me = lax.axis_index("ep")
    side = lax.rem(me, SPLIT)
    here = me // SPLIT
    partner = me + 1 - 2 * side
    rows, width = tokens.shape
    top = codes.shape[0]
    part = width // PARTS
    blocks = part // BLOCK
    chips = n // SPLIT
    slots = chips * CAP
    half_rows = chips * CAP
    tiled_rows = blocks * rows

    barrier = pltpu.get_barrier_semaphore()

    middle = chips // 2
    base = here // middle * middle

    def others(act, back=False):
        def across(step, carry):
            act(middle - base + lax.rem(here + (middle - step if back else step), middle))
            return carry

        def beside(step, carry):
            act(base + lax.rem(here + (middle - step if back else step), middle))
            return carry

        lax.fori_loop(0, middle, across, 0)
        lax.fori_loop(1, middle, beside, 0)

    def greet(q):
        pl.semaphore_signal(
            barrier, inc=1, device_id={"ep": q * SPLIT + side}, device_id_type=MESH
        )

    others(greet)
    pl.semaphore_signal(barrier, inc=1, device_id={"ep": partner}, device_id_type=MESH)

    fetch = pltpu.make_async_copy(tokens_hbm, tokens, rows_s)
    loads = [
        pltpu.make_async_copy(src.at[0], dst, wsem.at[i])
        for i, (src, dst) in enumerate(((wg_hbm, wg), (wu_hbm, wu), (wd_hbm, wd)))
    ]
    fetch.start()

    shape = (rows, tiled_rows)
    token_of = mod(iota(shape, 1), rows)
    repeat = one_hot(token_of == iota(shape, 0))
    earlier = one_hot(iota(shape, 0) < token_of)
    packet_rows = chips * TILE
    shape = (packet_rows, slots)
    line = iota(shape, 0)
    spread = one_hot(over(line, TILE) * CAP + mod(line, CAP) == iota(shape, 1))
    shape = (packet_rows, tiled_rows)
    in_block = over(mod(iota(shape, 0), TILE), CAP) == over(iota(shape, 1), rows)
    shape = (slots, tiled_rows)
    expert_of = over(iota(shape, 0), CAP).astype(F32)
    copy_of = mod(iota(shape, 0), CAP).astype(F32)
    ints = jnp.concatenate([codes[...] >> 8, codes[...] & 255], axis=0).astype(F32).astype(BF16)
    tiled = mm(ints, repeat)
    named = jnp.zeros(shape, F32)
    weight = jnp.zeros(shape, F32)
    for k in range(top):
        hit = tiled[k : k + 1] == expert_of
        named = jnp.where(hit, 1.0, named)
        weight = jnp.where(hit, tiled[top + k : top + k + 1], weight)
    place = mm(named[:, :rows].astype(BF16), earlier)
    chosen = jnp.where(place == copy_of, named, 0.0)

    pick = jnp.where(in_block, mm(spread, chosen.astype(BF16)), 0.0).astype(BF16)

    def outgoing(h, q):
        return pltpu.make_async_remote_copy(
            src_ref=send.at[h, q], dst_ref=recv.at[h, here], send_sem=send_s.at[h, q],
            recv_sem=send_r.at[h, here], device_id={"ep": q * SPLIT + side}, device_id_type=MESH,
        )

    def incoming(h, q):
        return pltpu.make_async_remote_copy(
            src_ref=send.at[h, q], dst_ref=recv.at[h, q], send_sem=send_s.at[h, q],
            recv_sem=send_r.at[h, q], device_id={"ep": q * SPLIT + side}, device_id_type=MESH,
        )

    def relay(h, q):
        return pltpu.make_async_remote_copy(
            src_ref=recv.at[h, q], dst_ref=relayed.at[h, q], send_sem=relay_s.at[h, q],
            recv_sem=relay_r.at[h, q], device_id={"ep": partner}, device_id_type=MESH,
        )

    fetch.wait()
    for load in loads:
        load.start()
    for h in range(PARTS):
        stacked = jnp.concatenate(
            [tokens[:, h * part + b * BLOCK : h * part + (b + 1) * BLOCK] for b in range(blocks)],
            axis=0,
        )
        send[h] = mm(pick, stacked).astype(BF16).reshape(chips, TILE, BLOCK)
        if h == 0:
            pl.semaphore_wait(barrier, chips)
        others(lambda q: outgoing(h, q).start())
    for h in range(PARTS):
        recv[h, here] = send[h, here]
        relay(h, here).start()

    gather[...] = packet_map((blocks * group * CAP, group * TILE), group, 0)
    scatter[...] = packet_map((group * TILE, blocks * group * CAP), group, 1)
    scaled = (chosen * weight * (1.0 / 256.0)).astype(BF16)
    pick_scaled = jnp.where(in_block, mm(spread, scaled), 0.0).astype(BF16)
    shape = (tiled_rows, tiled_rows)
    mix[...] = mm_nt(one_hot(iota(shape, 0) == iota(shape, 1)), pick_scaled).astype(BF16)

    def unpack(ref, h):
        parts = []
        step = group * CAP
        for g in range(chips // group):
            flat = ref[h, g * group : (g + 1) * group].reshape(group * TILE, BLOCK)
            tall = mm(gather[...], flat).astype(BF16)
            parts.append(
                jnp.concatenate([tall[b * step : (b + 1) * step] for b in range(blocks)], axis=1)
            )
        return parts

    for h in range(PARTS):

        def pass_on(q):
            incoming(h, q).wait_recv()
            relay(h, q).start()

        others(pass_on, back=True)

    loads[0].wait()
    loads[1].wait()
    gate_part = up_part = None
    for h in range(PARTS):
        relay(h, here).wait_recv()
        others(lambda q: relay(h, q).wait_recv(), back=True)
        x = jnp.concatenate(unpack(recv, h) + unpack(relayed, h), axis=0)
        gate_more = mm(x, wg[h * part : (h + 1) * part])
        up_more = mm(x, wu[h * part : (h + 1) * part])
        gate_part = gate_more if h == 0 else gate_part + gate_more
        up_part = up_more if h == 0 else up_part + up_more
    hidden = (gate_part / (1.0 + jnp.exp(-gate_part)) * up_part).astype(BF16)

    def exchange(h):
        return pltpu.make_async_remote_copy(
            src_ref=zsend.at[h], dst_ref=zrecv.at[h], send_sem=z_s.at[h], recv_sem=z_r.at[h],
            device_id={"ep": partner}, device_id_type=MESH,
        )

    def give_back(h, q):
        return pltpu.make_async_remote_copy(
            src_ref=rsend.at[h, q], dst_ref=ret.at[h, here], send_sem=ret_s.at[h, q],
            recv_sem=ret_r.at[h, here], device_id={"ep": q * SPLIT + side}, device_id_type=MESH,
        )

    def given(h, q):
        return pltpu.make_async_remote_copy(
            src_ref=rsend.at[h, q], dst_ref=ret.at[h, q], send_sem=ret_s.at[h, q],
            recv_sem=ret_r.at[h, q], device_id={"ep": q * SPLIT + side}, device_id_type=MESH,
        )

    loads[2].wait()
    for h in range(PARTS):
        z = mm(hidden, wd[:, h * part : (h + 1) * part])
        zsend[h] = z[half_rows:]
        exchange(h).start()
        kept[h] = z[:half_rows]
    for h in range(PARTS):
        exchange(h).wait_recv()
        total = (kept[h] + zrecv[h]).astype(BF16)
        for g in range(chips // group):
            lines = slice(g * group * CAP, (g + 1) * group * CAP)
            tall = jnp.concatenate(
                [total[lines, b * BLOCK : (b + 1) * BLOCK] for b in range(blocks)], axis=0
            )
            packed = mm(scatter[...], tall).astype(BF16)
            rsend[h, g * group : (g + 1) * group] = packed.reshape(group, TILE, BLOCK)
        others(lambda q: give_back(h, q).start())
        ret[h, here] = rsend[h, here]

    for h in range(PARTS):

        def sent(q):
            outgoing(h, q).wait_send()
            relay(h, q).wait_send()

        others(sent)
        relay(h, here).wait_send()
        exchange(h).wait_send()
    for h in range(PARTS):
        others(lambda q: given(h, q).wait_recv(), back=True)
        tall = mm(mix[...], ret[h].reshape(packet_rows, BLOCK)).astype(BF16)
        for b in range(blocks):
            at = h * part + b * BLOCK
            out[:, at : at + BLOCK] = tall[b * rows : (b + 1) * rows]
    for h in range(PARTS):
        others(lambda q: give_back(h, q).wait_send())


def shards(tokens, routes, gate_num, w_gate, w_up, w_down):
    n = lax.axis_size("ep")
    rows, width = tokens.shape
    chips = n // SPLIT
    part = width // PARTS
    blocks = part // BLOCK
    group = min(chips, 8)
    half_rows = chips * CAP
    codes = routes.T * 256 + gate_num.T
    vmem = pl.BlockSpec(memory_space=pltpu.VMEM)
    hbm = pl.BlockSpec(memory_space=pl.ANY)
    sems = pltpu.SemaphoreType.DMA
    return pl.pallas_call(
        functools.partial(kernel, n, group),
        out_shape=jax.ShapeDtypeStruct((rows, width), BF16),
        in_specs=[hbm, vmem, hbm, hbm, hbm],
        out_specs=vmem,
        scratch_shapes=[
            pltpu.VMEM((rows, width), BF16),
            pltpu.VMEM(w_gate.shape[1:], BF16),
            pltpu.VMEM(w_up.shape[1:], BF16),
            pltpu.VMEM(w_down.shape[1:], BF16),
            pltpu.VMEM((PARTS, chips, TILE, BLOCK), BF16),
            pltpu.VMEM((PARTS, chips, TILE, BLOCK), BF16),
            pltpu.VMEM((PARTS, chips, TILE, BLOCK), BF16),
            pltpu.VMEM((PARTS, half_rows, part), F32),
            pltpu.VMEM((PARTS, half_rows, part), F32),
            pltpu.VMEM((PARTS, half_rows, part), F32),
            pltpu.VMEM((PARTS, chips, TILE, BLOCK), BF16),
            pltpu.VMEM((PARTS, chips, TILE, BLOCK), BF16),
            pltpu.VMEM((blocks * group * CAP, group * TILE), BF16),
            pltpu.VMEM((group * TILE, blocks * group * CAP), BF16),
            pltpu.VMEM((blocks * rows, chips * TILE), BF16),
            sems,
            sems((3,)),
            sems((PARTS, chips)), sems((PARTS, chips)),
            sems((PARTS, chips)), sems((PARTS, chips)),
            sems((PARTS,)), sems((PARTS,)),
            sems((PARTS, chips)), sems((PARTS, chips)),
        ],
        compiler_params=pltpu.CompilerParams(
            collective_id=0, has_side_effects=True, vmem_limit_bytes=54800 << 10
        ),
    )(tokens, codes, w_gate, w_up, w_down)

def solution(mesh):
    return jax.shard_map(
        shards,
        mesh=mesh,
        in_specs=(
            P(("groups", "ep"), None),
            P(("groups", "ep"), None),
            P(("groups", "ep"), None),
            P("ep", None, None),
            P("ep", None, None),
            P("ep", None, None),
        ),
        out_specs=P(("groups", "ep"), None),
        check_vma=False,
    )
```

```python
import functools

import jax
import jax.numpy as jnp
from jax import lax
from jax.experimental import pallas as pl
from jax.experimental.pallas import tpu as pltpu
from jax.sharding import PartitionSpec as P

SPLIT = 2
CAP = 2
BLOCK = 256
PARTS = 2
TILE = 16
F32 = jnp.float32
BF16 = jnp.bfloat16
MESH = pl.DeviceIdType.MESH


def iota(shape, dim):
    return lax.broadcasted_iota(jnp.int32, shape, dim)


def over(x, k):
    return x >> (k.bit_length() - 1) if k & (k - 1) == 0 else x // k


def mod(x, k):
    return x & (k - 1) if k & (k - 1) == 0 else x - x // k * k


def mm(a, b):
    return jnp.dot(a, b, preferred_element_type=F32)


def mm_nt(a, b):
    return lax.dot_general(a, b, (((1,), (1,)), ((), ())), preferred_element_type=F32)


def one_hot(cond):
    return jnp.where(cond, 1.0, 0.0).astype(BF16)


def packet_map(shape, group, line_dim):
    line, col = iota(shape, line_dim), iota(shape, 1 - line_dim)
    row = mod(line, group * CAP)
    return one_hot(col == over(row, CAP) * TILE + over(line, group * CAP) * CAP + mod(row, CAP))


def kernel(
    n, group, tokens_hbm, codes, wg_hbm, wu_hbm, wd_hbm, out,
    tokens, wg, wu, wd, send, recv, relayed, kept, zsend, zrecv, rsend, ret, gather, scatter,
    mix, rows_s, wsem, send_s, send_r, relay_s, relay_r, z_s, z_r, ret_s, ret_r,
):
    me = lax.axis_index("ep")
    side = lax.rem(me, SPLIT)
    here = me // SPLIT
    partner = me + 1 - 2 * side
    rows, width = tokens.shape
    top = codes.shape[0]
    part = width // PARTS
    blocks = part // BLOCK
    chips = n // SPLIT
    slots = chips * CAP
    half_rows = chips * CAP
    tiled_rows = blocks * rows

    barrier = pltpu.get_barrier_semaphore()

    middle = chips // 2
    base = here // middle * middle

    def others(act, back=False):
        def across(step, carry):
            act(middle - base + lax.rem(here + (middle - step if back else step), middle))
            return carry

        def beside(step, carry):
            act(base + lax.rem(here + (middle - step if back else step), middle))
            return carry

        lax.fori_loop(0, middle, across, 0)
        lax.fori_loop(1, middle, beside, 0)

    def greet(q):
        pl.semaphore_signal(
            barrier, inc=1, device_id={"ep": q * SPLIT + side}, device_id_type=MESH
        )

    others(greet)
    pl.semaphore_signal(barrier, inc=1, device_id={"ep": partner}, device_id_type=MESH)

    fetch = pltpu.make_async_copy(tokens_hbm, tokens, rows_s)
    loads = [
        pltpu.make_async_copy(src.at[0], dst, wsem.at[i])
        for i, (src, dst) in enumerate(((wg_hbm, wg), (wu_hbm, wu), (wd_hbm, wd)))
    ]
    fetch.start()

    shape = (rows, tiled_rows)
    token_of = mod(iota(shape, 1), rows)
    repeat = one_hot(token_of == iota(shape, 0))
    earlier = one_hot(iota(shape, 0) < token_of)
    packet_rows = chips * TILE
    shape = (packet_rows, slots)
    line = iota(shape, 0)
    spread = one_hot(over(line, TILE) * CAP + mod(line, CAP) == iota(shape, 1))
    shape = (packet_rows, tiled_rows)
    in_block = over(mod(iota(shape, 0), TILE), CAP) == over(iota(shape, 1), rows)
    shape = (slots, tiled_rows)
    expert_of = over(iota(shape, 0), CAP).astype(F32)
    copy_of = mod(iota(shape, 0), CAP).astype(F32)
    ints = jnp.concatenate([codes[...] >> 8, codes[...] & 255], axis=0).astype(F32).astype(BF16)
    tiled = mm(ints, repeat)
    named = jnp.zeros(shape, F32)
    weight = jnp.zeros(shape, F32)
    for k in range(top):
        hit = tiled[k : k + 1] == expert_of
        named = jnp.where(hit, 1.0, named)
        weight = jnp.where(hit, tiled[top + k : top + k + 1], weight)
    place = mm(named[:, :rows].astype(BF16), earlier)
    chosen = jnp.where(place == copy_of, named, 0.0)

    pick = jnp.where(in_block, mm(spread, chosen.astype(BF16)), 0.0).astype(BF16)

    def outgoing(h, q):
        return pltpu.make_async_remote_copy(
            src_ref=send.at[h, q], dst_ref=recv.at[h, here], send_sem=send_s.at[h, q],
            recv_sem=send_r.at[h, here], device_id={"ep": q * SPLIT + side}, device_id_type=MESH,
        )

    def incoming(h, q):
        return pltpu.make_async_remote_copy(
            src_ref=send.at[h, q], dst_ref=recv.at[h, q], send_sem=send_s.at[h, q],
            recv_sem=send_r.at[h, q], device_id={"ep": q * SPLIT + side}, device_id_type=MESH,
        )

    def relay(h, q):
        return pltpu.make_async_remote_copy(
            src_ref=recv.at[h, q], dst_ref=relayed.at[h, q], send_sem=relay_s.at[h, q],
            recv_sem=relay_r.at[h, q], device_id={"ep": partner}, device_id_type=MESH,
        )

    fetch.wait()
    for load in loads:
        load.start()
    for h in range(PARTS):
        stacked = jnp.concatenate(
            [tokens[:, h * part + b * BLOCK : h * part + (b + 1) * BLOCK] for b in range(blocks)],
            axis=0,
        )
        send[h] = mm(pick, stacked).astype(BF16).reshape(chips, TILE, BLOCK)
        if h == 0:
            pl.semaphore_wait(barrier, chips)
        others(lambda q: outgoing(h, q).start())
    for h in range(PARTS):
        recv[h, here] = send[h, here]
        relay(h, here).start()

    gather[...] = packet_map((blocks * group * CAP, group * TILE), group, 0)
    scatter[...] = packet_map((group * TILE, blocks * group * CAP), group, 1)
    scaled = (chosen * weight * (1.0 / 256.0)).astype(BF16)
    pick_scaled = jnp.where(in_block, mm(spread, scaled), 0.0).astype(BF16)
    shape = (tiled_rows, tiled_rows)
    mix[...] = mm_nt(one_hot(iota(shape, 0) == iota(shape, 1)), pick_scaled).astype(BF16)

    def unpack(ref, h):
        parts = []
        step = group * CAP
        for g in range(chips // group):
            flat = ref[h, g * group : (g + 1) * group].reshape(group * TILE, BLOCK)
            tall = mm(gather[...], flat).astype(BF16)
            parts.append(
                jnp.concatenate([tall[b * step : (b + 1) * step] for b in range(blocks)], axis=1)
            )
        return parts

    for h in range(PARTS):

        def pass_on(q):
            incoming(h, q).wait_recv()
            relay(h, q).start()

        others(pass_on, back=True)

    loads[0].wait()
    loads[1].wait()
    gate_part = up_part = None
    for h in range(PARTS):
        relay(h, here).wait_recv()
        others(lambda q: relay(h, q).wait_recv(), back=True)
        x = jnp.concatenate(unpack(recv, h) + unpack(relayed, h), axis=0)
        gate_more = mm(x, wg[h * part : (h + 1) * part])
        up_more = mm(x, wu[h * part : (h + 1) * part])
        gate_part = gate_more if h == 0 else gate_part + gate_more
        up_part = up_more if h == 0 else up_part + up_more
    hidden = (gate_part / (1.0 + jnp.exp(-gate_part)) * up_part).astype(BF16)

    def exchange(h):
        return pltpu.make_async_remote_copy(
            src_ref=zsend.at[h], dst_ref=zrecv.at[h], send_sem=z_s.at[h], recv_sem=z_r.at[h],
            device_id={"ep": partner}, device_id_type=MESH,
        )

    def give_back(h, q):
        return pltpu.make_async_remote_copy(
            src_ref=rsend.at[h, q], dst_ref=ret.at[h, here], send_sem=ret_s.at[h, q],
            recv_sem=ret_r.at[h, here], device_id={"ep": q * SPLIT + side}, device_id_type=MESH,
        )

    def given(h, q):
        return pltpu.make_async_remote_copy(
            src_ref=rsend.at[h, q], dst_ref=ret.at[h, q], send_sem=ret_s.at[h, q],
            recv_sem=ret_r.at[h, q], device_id={"ep": q * SPLIT + side}, device_id_type=MESH,
        )

    loads[2].wait()
    for h in range(PARTS):
        z = mm(hidden, wd[:, h * part : (h + 1) * part])
        zsend[h] = z[half_rows:].astype(BF16)
        exchange(h).start()
        kept[h] = z[:half_rows]
    for h in range(PARTS):
        exchange(h).wait_recv()
        total = (kept[h] + zrecv[h].astype(F32)).astype(BF16)
        for g in range(chips // group):
            lines = slice(g * group * CAP, (g + 1) * group * CAP)
            tall = jnp.concatenate(
                [total[lines, b * BLOCK : (b + 1) * BLOCK] for b in range(blocks)], axis=0
            )
            packed = mm(scatter[...], tall).astype(BF16)
            rsend[h, g * group : (g + 1) * group] = packed.reshape(group, TILE, BLOCK)
        others(lambda q: give_back(h, q).start())
        ret[h, here] = rsend[h, here]

    for h in range(PARTS):

        def sent(q):
            outgoing(h, q).wait_send()
            relay(h, q).wait_send()

        others(sent)
        relay(h, here).wait_send()
        exchange(h).wait_send()
    for h in range(PARTS):
        others(lambda q: given(h, q).wait_recv(), back=True)
        tall = mm(mix[...], ret[h].reshape(packet_rows, BLOCK)).astype(BF16)
        for b in range(blocks):
            at = h * part + b * BLOCK
            out[:, at : at + BLOCK] = tall[b * rows : (b + 1) * rows]
    for h in range(PARTS):
        others(lambda q: give_back(h, q).wait_send())


def shards(tokens, routes, gate_num, w_gate, w_up, w_down):
    n = lax.axis_size("ep")
    rows, width = tokens.shape
    chips = n // SPLIT
    part = width // PARTS
    blocks = part // BLOCK
    group = min(chips, 8)
    half_rows = chips * CAP
    codes = routes.T * 256 + gate_num.T
    vmem = pl.BlockSpec(memory_space=pltpu.VMEM)
    hbm = pl.BlockSpec(memory_space=pl.ANY)
    sems = pltpu.SemaphoreType.DMA
    return pl.pallas_call(
        functools.partial(kernel, n, group),
        out_shape=jax.ShapeDtypeStruct((rows, width), BF16),
        in_specs=[hbm, vmem, hbm, hbm, hbm],
        out_specs=vmem,
        scratch_shapes=[
            pltpu.VMEM((rows, width), BF16),
            pltpu.VMEM(w_gate.shape[1:], BF16),
            pltpu.VMEM(w_up.shape[1:], BF16),
            pltpu.VMEM(w_down.shape[1:], BF16),
            pltpu.VMEM((PARTS, chips, TILE, BLOCK), BF16),
            pltpu.VMEM((PARTS, chips, TILE, BLOCK), BF16),
            pltpu.VMEM((PARTS, chips, TILE, BLOCK), BF16),
            pltpu.VMEM((PARTS, half_rows, part), F32),
            pltpu.VMEM((PARTS, half_rows, part), BF16),
            pltpu.VMEM((PARTS, half_rows, part), BF16),
            pltpu.VMEM((PARTS, chips, TILE, BLOCK), BF16),
            pltpu.VMEM((PARTS, chips, TILE, BLOCK), BF16),
            pltpu.VMEM((blocks * group * CAP, group * TILE), BF16),
            pltpu.VMEM((group * TILE, blocks * group * CAP), BF16),
            pltpu.VMEM((blocks * rows, chips * TILE), BF16),
            sems,
            sems((3,)),
            sems((PARTS, chips)), sems((PARTS, chips)),
            sems((PARTS, chips)), sems((PARTS, chips)),
            sems((PARTS,)), sems((PARTS,)),
            sems((PARTS, chips)), sems((PARTS, chips)),
        ],
        compiler_params=pltpu.CompilerParams(
            collective_id=0, has_side_effects=True, vmem_limit_bytes=54800 << 10
        ),
    )(tokens, codes, w_gate, w_up, w_down)

def solution(mesh):
    return jax.shard_map(
        shards,
        mesh=mesh,
        in_specs=(
            P(("groups", "ep"), None),
            P(("groups", "ep"), None),
            P(("groups", "ep"), None),
            P("ep", None, None),
            P("ep", None, None),
            P("ep", None, None),
        ),
        out_specs=P(("groups", "ep"), None),
        check_vma=False,
    )
```
